128 devices in a mesh: rep: 2 (over y_lo), fsdp: 8 (over z, y_hi), tp: 8 (over x, core).
Axes of the slice: x: 4, y: 4 (y_hi: 2, y_lo: 2; y = y_hi * 2 + y_lo), z: 4, core: 2. Of those that a mesh axis runs over, the one named last changes fastest.
Arguments:
- images: bfloat16 [16, 577, 1024], P(('rep', 'fsdp')), may hold values from -6 to 6
- cotangent: bfloat16 [16, 577, 1024], P(('rep', 'fsdp')), may hold values from -6 to 6
- norm1_gain: float32 [2, 1024], replicated, may hold values from 0.1 to 1.9
- norm1_shift: float32 [2, 1024], replicated, may hold values from -3 to 3
- qkv_weight: bfloat16 [2, 1024, 3, 1024], P(None, 'fsdp', None, 'tp'), may hold values from -0.1875 to 0.1875
- qv_bias: float32 [2, 2, 1024], P(None, None, 'tp'), may hold values from -3 to 3
- out_weight: bfloat16 [2, 1024, 1024], P(None, 'tp', 'fsdp'), may hold values from -0.75 to 0.75
- out_bias: float32 [2, 1024], replicated, may hold values from -3 to 3
- norm2_gain: float32 [2, 1024], replicated, may hold values from 0.1 to 1.9
- norm2_shift: float32 [2, 1024], replicated, may hold values from -3 to 3
- up_weight: bfloat16 [2, 1024, 4096], P(None, 'fsdp', 'tp'), may hold values from -0.1875 to 0.1875
- up_bias: float32 [2, 4096], P(None, 'tp'), may hold values from -3 to 3
- down_weight: bfloat16 [2, 4096, 1024], P(None, 'tp', 'fsdp'), may hold values from -0.09375 to 0.09375
- down_bias: float32 [2, 1024], replicated, may hold values from -5 to 5
Outputs:
- out_act: float32 [16, 577, 1024], P(('rep', 'fsdp'))
- grad_images: float32 [16, 577, 1024], P(('rep', 'fsdp'))
- grad_norm1_gain: float32 [2, 1024], replicated
- grad_norm1_shift: float32 [2, 1024], replicated
- grad_qkv_weight: float32 [2, 1024, 3, 1024], P(None, 'fsdp', None, 'tp')
- grad_qv_bias: float32 [2, 2, 1024], P(None, None, 'tp')
- grad_out_weight: float32 [2, 1024, 1024], P(None, 'tp', 'fsdp')
- grad_out_bias: float32 [2, 1024], replicated
- grad_norm2_gain: float32 [2, 1024], replicated
- grad_norm2_shift: float32 [2, 1024], replicated
- grad_up_weight: float32 [2, 1024, 4096], P(None, 'fsdp', 'tp')
- grad_up_bias: float32 [2, 4096], P(None, 'tp')
- grad_down_weight: float32 [2, 4096, 1024], P(None, 'tp', 'fsdp')
- grad_down_bias: float32 [2, 1024], replicated
The draws below stay inside these ranges and needn't reach their ends.
All inputs are finite; a program needn't handle non-finite values.
Results may differ from the reference program's by a relative error of at most 0.012.
Values may be sent and summed in bfloat16 or wider, within the bound.
No kernel may reach another device: no remote copies, remote signals or barrier semaphores. Data moves between devices by JAX's collectives and lax.ppermute only.
A program may use at most 128 MiB of HBM per device.

```python
import jax
import jax.numpy as jnp
from jax import lax

D = 1024
HEADS = 16
HEAD_DIM = 64
FF = 4096
SEQ = 577
LAYERS = 2
IMAGES = 16
N_TP = 8


def shard_levels(rng, dims, cuts, least, high):
    def one(dim, parts):
        heights = jax.random.uniform(jax.random.fold_in(jax.random.fold_in(rng, 6), dim), (parts,), jnp.float32, least / len(cuts), high / len(cuts))
        return jnp.repeat(jnp.exp(heights), dims[dim] // parts).reshape((-1,) + (1,) * (len(dims) - dim - 1))

    loudness = one(*cuts[0])
    for cut in cuts[1:]:
        loudness = loudness * one(*cut)
    return loudness


def bell_draw(rng, shape, scale, bound, shards=(), dtype=jnp.bfloat16):
    result = jax.random.normal(rng, shape, jnp.float32) * scale
    if len(shards) > 0:
        result = shard_levels(rng, shape, shards, -0.22, 0.18) * result
    return jnp.clip(result, min=-bound, max=bound).astype(dtype)


def setup_inputs(seed: int = 0) -> dict:
    keys = jax.random.split(jax.random.key(seed), 15)
    return {
        "images": bell_draw(keys[0], (IMAGES, SEQ, D), 1.0, 6.0, ((0, 16),)),
        "cotangent": bell_draw(keys[1], (IMAGES, SEQ, D), 1.0, 6.0, ((0, 16),)),
        "norm1_gain": jnp.clip(1.0 + 0.18 * jax.random.normal(keys[2], (LAYERS, D), jnp.float32), 0.1, 1.9),
        "norm1_shift": bell_draw(keys[3], (LAYERS, D), 0.5, 3.0, (), jnp.float32),
        "qkv_weight": bell_draw(keys[4], (LAYERS, D, 3, D), D ** -0.5, 0.1875, ((1, 8), (3, 8))),
        "qv_bias": bell_draw(keys[5], (LAYERS, 2, D), 0.5, 3.0, ((2, 8),), jnp.float32),
        "out_weight": bell_draw(keys[6], (LAYERS, D, D), (D // 16) ** -0.5, 0.75, ((1, 8), (2, 8))),
        "out_bias": bell_draw(keys[7], (LAYERS, D), 0.5, 3.0, (), jnp.float32),
        "norm2_gain": jnp.clip(1.0 + 0.18 * jax.random.normal(keys[8], (LAYERS, D), jnp.float32), 0.1, 1.9),
        "norm2_shift": bell_draw(keys[9], (LAYERS, D), 0.5, 3.0, (), jnp.float32),
        "up_weight": bell_draw(keys[10], (LAYERS, D, FF), D ** -0.5, 0.1875, ((1, 8), (2, 8))),
        "up_bias": bell_draw(keys[11], (LAYERS, FF), 0.5, 3.0, ((1, 8),), jnp.float32),
        "down_weight": bell_draw(keys[12], (LAYERS, FF, D), FF ** -0.5, 0.09375, ((1, 8), (2, 8))),
        "down_bias": bell_draw(keys[13], (LAYERS, D), 0.8, 5.0, (), jnp.float32),
    }


EPSILON = 1e-05

def norm_forward(values_in, norm_gain, norm_shift):
    row_mean = lax.optimization_barrier(jnp.mean(values_in, -1, keepdims=True))
    centred = values_in - row_mean
    inv_std = lax.rsqrt(lax.optimization_barrier(jnp.mean(centred * centred, -1, keepdims=True)) + EPSILON)
    normed = centred * inv_std
    return (normed * norm_gain + norm_shift, normed, inv_std)

def norm_backward(upstream, normed, inv_std, norm_gain):
    scaled = upstream * norm_gain
    return inv_std * (scaled - lax.optimization_barrier(jnp.mean(scaled, -1, keepdims=True)) - normed * lax.optimization_barrier(jnp.mean(scaled * normed, -1, keepdims=True)))

def gelu_parts(pre_act):
    normal_cdf = 0.5 * (1.0 + lax.erf(pre_act * 0.7071067811865476))
    normal_pdf = jnp.exp(-0.5 * pre_act * pre_act) * 0.3989422804014327
    return (pre_act * normal_cdf, normal_cdf + pre_act * normal_pdf)

def attend(queries, key_vecs, val_vecs):
    softmax_scale = HEAD_DIM ** (-0.5)
    scores = jnp.einsum('qhe,khe->hqk', queries.astype(jnp.float32), key_vecs.astype(jnp.float32)) * softmax_scale
    row_max = lax.optimization_barrier(jnp.max(scores, -1, keepdims=True))
    log_total = row_max + jnp.log(lax.optimization_barrier(jnp.sum(jnp.exp(scores - row_max), -1, keepdims=True)))
    prob_b = jnp.exp(scores - log_total).astype(jnp.bfloat16)
    mixed_b = jnp.einsum('hqk,khe->qhe', prob_b.astype(jnp.float32), val_vecs.astype(jnp.float32)).astype(jnp.bfloat16)
    return (mixed_b, log_total)

def attend_back(queries, key_vecs, val_vecs, log_total, d_mixed):
    softmax_scale = HEAD_DIM ** (-0.5)
    scores = jnp.einsum('qhe,khe->hqk', queries.astype(jnp.float32), key_vecs.astype(jnp.float32)) * softmax_scale
    probs = jnp.exp(scores - log_total)
    prob_b = probs.astype(jnp.bfloat16)
    d_values = jnp.einsum('hqk,qhe->khe', prob_b.astype(jnp.float32), d_mixed.astype(jnp.float32))
    d_probs = jnp.einsum('qhe,khe->hqk', d_mixed.astype(jnp.float32), val_vecs.astype(jnp.float32))
    row_dot = lax.optimization_barrier(jnp.sum(probs * d_probs, -1, keepdims=True))
    d_scores = (probs * (d_probs - row_dot) * softmax_scale).astype(jnp.bfloat16).astype(jnp.float32)
    d_queries = jnp.einsum('hqk,khe->qhe', d_scores, key_vecs.astype(jnp.float32))
    d_keys = jnp.einsum('hqk,qhe->khe', d_scores, queries.astype(jnp.float32))
    return (d_queries, d_keys, d_values)

def image_pass(one_image, one_cot, params):
    gain_one, shift_one, qkv_all, bias_qv, out_all, bias_out, gain_two, shift_two, up_all, bias_up, down_all, bias_down = params
    group_count = N_TP
    col_width = D // group_count
    unit_width = FF // group_count
    heads_group = HEADS // group_count
    state = one_image.astype(jnp.float32)
    saved = []
    for layer_idx in range(LAYERS):
        normed_a, unit_a, inv_a = norm_forward(state, gain_one[layer_idx], shift_one[layer_idx])
        first_b = normed_a.astype(jnp.bfloat16)
        attn_total = jnp.zeros((SEQ, D), jnp.float32)
        attn_parts = []
        for group_idx in range(group_count):
            col_range = slice(group_idx * col_width, (group_idx + 1) * col_width)
            projected = jnp.einsum('rd,dtc->rtc', first_b.astype(jnp.float32), qkv_all[layer_idx][:, :, col_range].astype(jnp.float32))
            queries = (projected[:, 0] + bias_qv[layer_idx, 0, col_range]).astype(jnp.bfloat16).reshape(SEQ, heads_group, HEAD_DIM)
            key_vecs = projected[:, 1].astype(jnp.bfloat16).reshape(SEQ, heads_group, HEAD_DIM)
            val_vecs = (projected[:, 2] + bias_qv[layer_idx, 1, col_range]).astype(jnp.bfloat16).reshape(SEQ, heads_group, HEAD_DIM)
            mixed_b, log_total = attend(queries, key_vecs, val_vecs)
            mixed_flat = mixed_b.reshape(SEQ, col_width)
            attn_total = attn_total + jnp.dot(mixed_flat, out_all[layer_idx][col_range, :], preferred_element_type=jnp.float32)
            attn_parts.append((queries, key_vecs, val_vecs, log_total, mixed_flat))
        middle = state + attn_total + bias_out[layer_idx]
        normed_b, unit_b, inv_b = norm_forward(middle, gain_two[layer_idx], shift_two[layer_idx])
        second_b = normed_b.astype(jnp.bfloat16)
        mlp_total = jnp.zeros((SEQ, D), jnp.float32)
        mlp_parts = []
        for group_idx in range(group_count):
            unit_range = slice(group_idx * unit_width, (group_idx + 1) * unit_width)
            hidden = jnp.dot(second_b, up_all[layer_idx][:, unit_range], preferred_element_type=jnp.float32) + bias_up[layer_idx, unit_range]
            active, slopes = gelu_parts(hidden)
            active_b = active.astype(jnp.bfloat16)
            mlp_total = mlp_total + jnp.dot(active_b, down_all[layer_idx][unit_range, :], preferred_element_type=jnp.float32)
            mlp_parts.append((active_b, slopes))
        saved.append((unit_a, inv_a, first_b, attn_parts, unit_b, inv_b, second_b, mlp_parts))
        state = middle + mlp_total + bias_down[layer_idx]
    gradient = one_cot.astype(jnp.float32)
    per_layer = [None] * LAYERS
    for layer_idx in reversed(range(LAYERS)):
        unit_a, inv_a, first_b, attn_parts, unit_b, inv_b, second_b, mlp_parts = saved[layer_idx]
        d_down_bias = lax.optimization_barrier(jnp.sum(gradient, 0))
        grad_b = gradient.astype(jnp.bfloat16)
        d_norm_two = jnp.zeros((SEQ, D), jnp.float32)
        down_pieces, up_pieces, up_bias_pieces = ([], [], [])
        for group_idx in range(group_count):
            unit_range = slice(group_idx * unit_width, (group_idx + 1) * unit_width)
            active_b, slopes = mlp_parts[group_idx]
            down_pieces.append(jnp.dot(active_b.T, grad_b, preferred_element_type=jnp.float32))
            d_hidden = jnp.dot(grad_b, down_all[layer_idx][unit_range, :].T, preferred_element_type=jnp.float32) * slopes
            up_bias_pieces.append(lax.optimization_barrier(jnp.sum(d_hidden, 0)))
            d_hidden_b = d_hidden.astype(jnp.bfloat16)
            up_pieces.append(jnp.dot(second_b.T, d_hidden_b, preferred_element_type=jnp.float32))
            d_norm_two = d_norm_two + jnp.dot(d_hidden_b, up_all[layer_idx][:, unit_range].T, preferred_element_type=jnp.float32)
        d_gain_two = lax.optimization_barrier(jnp.sum(d_norm_two * unit_b, 0))
        d_shift_two = lax.optimization_barrier(jnp.sum(d_norm_two, 0))
        grad_mid = gradient + norm_backward(d_norm_two, unit_b, inv_b, gain_two[layer_idx])
        d_out_bias = lax.optimization_barrier(jnp.sum(grad_mid, 0))
        mid_b = grad_mid.astype(jnp.bfloat16)
        d_norm_one = jnp.zeros((SEQ, D), jnp.float32)
        out_pieces, qkv_pieces, bias_pieces = ([], [], [])
        for group_idx in range(group_count):
            col_range = slice(group_idx * col_width, (group_idx + 1) * col_width)
            queries, key_vecs, val_vecs, log_total, mixed_flat = attn_parts[group_idx]
            out_pieces.append(jnp.dot(mixed_flat.T, mid_b, preferred_element_type=jnp.float32))
            d_mixed = jnp.dot(mid_b, out_all[layer_idx][col_range, :].T, preferred_element_type=jnp.float32).astype(jnp.bfloat16).reshape(SEQ, heads_group, HEAD_DIM)
            d_queries, d_keys, d_values = attend_back(queries, key_vecs, val_vecs, log_total, d_mixed)
            d_queries = d_queries.reshape(SEQ, col_width)
            d_keys = d_keys.reshape(SEQ, col_width)
            d_values = d_values.reshape(SEQ, col_width)
            bias_pieces.append(jnp.stack([lax.optimization_barrier(jnp.sum(d_queries, 0)), lax.optimization_barrier(jnp.sum(d_values, 0))]))
            d_proj_b = jnp.stack([d_queries, d_keys, d_values], 1).astype(jnp.bfloat16)
            qkv_pieces.append(jnp.einsum('rd,rtc->dtc', first_b.astype(jnp.float32), d_proj_b.astype(jnp.float32)))
            d_norm_one = d_norm_one + jnp.einsum('rtc,dtc->rd', d_proj_b.astype(jnp.float32), qkv_all[layer_idx][:, :, col_range].astype(jnp.float32))
        d_gain_one = lax.optimization_barrier(jnp.sum(d_norm_one * unit_a, 0))
        d_shift_one = lax.optimization_barrier(jnp.sum(d_norm_one, 0))
        gradient = grad_mid + norm_backward(d_norm_one, unit_a, inv_a, gain_one[layer_idx])
        per_layer[layer_idx] = (d_gain_one, d_shift_one, jnp.concatenate(qkv_pieces, 2), jnp.concatenate(bias_pieces, 1), jnp.concatenate(out_pieces, 0), d_out_bias, d_gain_two, d_shift_two, jnp.concatenate(up_pieces, 1), jnp.concatenate(up_bias_pieces, 0), jnp.concatenate(down_pieces, 0), d_down_bias)
    grads = tuple((jnp.stack([per_layer[layer_idx][member] for layer_idx in range(LAYERS)]) for member in range(12)))
    return (state, gradient, grads)

def reference(images, cotangent, norm1_gain, norm1_shift, qkv_weight, qv_bias, out_weight, out_bias, norm2_gain, norm2_shift, up_weight, up_bias, down_weight, down_bias):
    params = (norm1_gain, norm1_shift, qkv_weight, qv_bias, out_weight, out_bias, norm2_gain, norm2_shift, up_weight, up_bias, down_weight, down_bias)
    start = tuple((jnp.zeros(weight_arr.shape, jnp.float32) for weight_arr in params))

    def one_step(carry, pair):
        state, gradient, grads = image_pass(pair[0], pair[1], params)
        return (tuple((carry_arr + grad_arr for carry_arr, grad_arr in zip(carry, grads))), (state, gradient))
    totals, stacked = lax.scan(one_step, start, (images, cotangent))
    return (stacked[0], stacked[1], totals[0], totals[1], totals[2], totals[3], totals[4], totals[5], totals[6], totals[7], totals[8], totals[9], totals[10], totals[11])
```

```python
import jax
import jax.numpy as jnp
from jax import lax
from jax.experimental import pallas as pl
from jax.experimental.pallas import tpu as pltpu
from jax.sharding import PartitionSpec as P

F32, BF16 = jnp.float32, jnp.bfloat16
EPSILON = 1e-05
HEAD = 64
BLK = 80
ROWS = 4 * BLK
NEG = -1e30
MIB = 1 << 20


def call(kernel, outs, args, flops=0, scratch=(), smem=0, vmem=40, after=()):
    out_shape = [jax.ShapeDtypeStruct(sh, d) for sh, d in outs]
    specs, arrays, views = [], [], []
    for i, arg in enumerate(args):
        arr, *view = arg if isinstance(arg, tuple) else (arg,)
        place = next((n for n, seen in enumerate(arrays) if seen is arr), len(arrays))
        if place == len(arrays):
            arrays.append(arr)
            specs.append(pl.BlockSpec(memory_space=pltpu.SMEM if i < smem else pltpu.VMEM))
        views.append((place, view))
    nbytes = sum(a.size * a.dtype.itemsize for a in arrays)
    count = len(arrays)
    specs += [pl.BlockSpec(memory_space=pl.ANY)] * len(after)

    def run(*refs):
        ins = [
            refs[n].at[:, view[0] * view[1] : view[0] * (view[1] + 1)] if view else refs[n]
            for n, view in views
        ]
        kernel(*ins, *refs[count + len(after) :])

    return list(
        pl.pallas_call(
            run,
            out_shape=out_shape,
            in_specs=specs,
            out_specs=[pl.BlockSpec(memory_space=pltpu.VMEM)] * len(outs),
            scratch_shapes=list(scratch),
            compiler_params=pltpu.CompilerParams(vmem_limit_bytes=vmem * MIB),
            cost_estimate=pl.CostEstimate(flops=1024, bytes_accessed=1024, transcendentals=0),
        )(*arrays, *after)
    )


def nn(a, b):
    return lax.dot_general(a, b, (((1,), (0,)), ((), ())), preferred_element_type=F32)


def nt(a, b):
    return lax.dot_general(a, b, (((1,), (1,)), ((), ())), preferred_element_type=F32)


def tn(a, b):
    return lax.dot_general(a, b, (((0,), (0,)), ((), ())), preferred_element_type=F32)


def by_rows(a, pieces):
    total = None
    for j, w in enumerate(pieces):
        part = nn(a[:, 256 * j : 256 * j + 256], w[...])
        total = part if total is None else total + part
    return total


def norm(v):
    mean = jnp.mean(v, -1, keepdims=True)
    cen = v - mean
    inv = lax.rsqrt(jnp.mean(cen * cen, -1, keepdims=True) + EPSILON)
    return cen * inv, inv


def gelu(u):
    cdf = 0.5 * (1.0 + lax.erf(u * 0.7071067811865476))
    pdf = jnp.exp(-0.5 * u * u) * 0.3989422804014327
    return u * cdf, cdf + u * pdf


def columns(sc):
    return [pl.multiple_of((sc[2] ^ p) * 128, 128) for p in range(8)]


def prep_kernel(sc, img, cot, vec, a0, n0, h0, eb, vout, esum, ims):
    cols = columns(sc)
    for p, col in enumerate(cols):
        vout[:, 128 * p : 128 * p + 128] = vec[:, pl.ds(col, 128)]
    for j in range(4):
        row = pl.multiple_of((sc[0] * 4 + (sc[1] ^ j)) * BLK, BLK)
        for p, col in enumerate(cols):
            here = (slice(BLK * j, BLK * j + BLK), slice(128 * p, 128 * p + 128))
            there = (pl.ds(row, BLK), pl.ds(col, 128))
            ims[here] = img[there]
            eb[here] = cot[there]
    h0[...] = ims[0:BLK, :].astype(F32)
    esum[...] = jnp.sum(eb[0:BLK, :].astype(F32), 0, keepdims=True)
    gain, shift = vout[0:1, :], vout[2:3, :]
    for j in range(4):
        rows = slice(BLK * j, BLK * j + BLK)
        n, _ = norm(ims[rows, :].astype(F32))
        n0[rows, :] = n
        a0[rows, :] = (n * gain + shift).astype(BF16)


def gather_rows(parts, full):
    for j, part in enumerate(parts):
        full[BLK * j : BLK * j + BLK, :] = part[...]


def sides(refs):
    return refs[0:4], refs[4:8]


def send_rows(terms, mine, sends):
    for j in range(4):
        at = slice(256 * j, 256 * j + 256)
        total = None
        for x, pieces in terms:
            part = nt(x, pieces[j][...])
            total = part if total is None else total + part
        mine[:, at] = total[0:BLK, :]
        for i, send in enumerate(sends):
            send[:, at] = total[BLK * (i + 1) : BLK * (i + 2), :].astype(BF16)
        yield at, total


def send_parts(terms, mine, sends):
    for _ in send_rows(terms, mine, sends):
        pass


def qkv_kernel(nparts, *refs):
    parts, (wo, wp), (bo, bp), (q, kv), rest = (
        refs[:nparts],
        sides(refs[nparts : nparts + 8]),
        refs[nparts + 8 : nparts + 10],
        refs[nparts + 10 : nparts + 12],
        refs[nparts + 12 :],
    )
    a = parts[0]
    if nparts > 1:
        gather_rows(parts, rest[0])
        a = rest[0]
    for i, (w, b) in enumerate(((wo, bo), (wp, bp))):
        y = by_rows(a, w)
        at = slice(128 * i, 128 * i + 128)
        q[:, at] = (y[:, 0:128] + b[0:1, :]).astype(BF16)
        kv[:, at] = y[:, 128:256].astype(BF16)
        kv[:, 256 + 128 * i : 384 + 128 * i] = (y[:, 256:384] + b[1:2, :]).astype(BF16)


def swap128(ref):
    for i, j in enumerate((1, 0, 3, 2)):
        yield slice(128 * i, 128 * i + 128), slice(128 * j, 128 * j + 128)


def attn_kernel(q, kv, kvp, mask, *refs):
    wo, wp = sides(refs[:8])
    mixed, lse, kvf, mine, s1, s2, s3 = refs[8:]
    kvf[0:ROWS, :] = kv[...]
    for here, there in swap128(kvp):
        kvf[ROWS:, here] = kvp[:, there]
    for h in range(4):
        at = slice(HEAD * h, HEAD * h + HEAD)
        qh = q[:, at] * jnp.asarray(0.125, BF16)
        s = nt(qh, kvf[:, at]) + mask[...]
        top = jnp.max(s, -1, keepdims=True)
        e = jnp.exp(s - top)
        tot = jnp.sum(e, -1, keepdims=True)
        lse[:, h : h + 1] = top + jnp.log(tot)
        out = nn(e.astype(BF16), kvf[:, 256 + HEAD * h : 256 + HEAD * h + HEAD])
        mixed[:, at] = (out * (1.0 / tot)).astype(BF16)
    send_parts(((mixed[:, 0:128], wo), (mixed[:, 128:256], wp)), mine, (s1, s2, s3))


def ln_kernel(mine, r1, r2, r3, prev, bias, gain, shift, h, b):
    v = prev[...] + (
        (mine[...] + r1[...].astype(F32)) + (r2[...].astype(F32) + r3[...].astype(F32))
    ) + bias[...]
    h[...] = v
    n, _ = norm(v)
    b[...] = (n * gain[...] + shift[...]).astype(BF16)


def halves(x):
    return x[:, 0:512], x[:, 512:1024]


def mlp_kernel(b0, b1, b2, b3, *refs):
    ups, downs = sides(refs[:8]), sides(refs[8:16])
    bias, z, slope, bf, mine, s1, s2, s3 = refs[16:]
    gather_rows((b0, b1, b2, b3), bf)
    for i in range(2):
        at = slice(512 * i, 512 * i + 512)
        zz, sl = gelu(by_rows(bf, ups[i]) + bias[:, at])
        slope[:, at] = sl
        z[:, at] = zz.astype(BF16)
    send_parts(tuple(zip(halves(z), downs)), mine, (s1, s2, s3))


def mlp_turn_kernel(b0, b1, b2, b3, eb, *refs):
    ups, downs = sides(refs[:8]), sides(refs[8:16])
    bias, z, dub, bf, usum, mine, s1, s2, s3 = refs[16:]
    gather_rows((b0, b1, b2, b3), bf)
    for i in range(2):
        at = slice(512 * i, 512 * i + 512)
        zz, sl = gelu(by_rows(bf, ups[i]) + bias[:, at])
        z[:, at] = zz.astype(BF16)
        du = by_rows(eb, downs[i]) * sl
        usum[:, at] = jnp.sum(du, 0, keepdims=True)
        dub[:, at] = du.astype(BF16)
    send_parts(tuple(zip(halves(dub), ups)), mine, (s1, s2, s3))


def down_kernel(z, *refs):
    mine, s1, s2, s3 = refs[8:]
    send_parts(tuple(zip(halves(z), sides(refs[:8]))), mine, (s1, s2, s3))


def mlp_back_kernel(e0, e1, e2, e3, slope, *refs):
    ups, downs = sides(refs[:8]), sides(refs[8:16])
    dub, ebf, usum, mine, s1, s2, s3 = refs[16:]
    gather_rows((e0, e1, e2, e3), ebf)
    for i in range(2):
        at = slice(512 * i, 512 * i + 512)
        du = by_rows(ebf, downs[i]) * slope[:, at]
        usum[:, at] = jnp.sum(du, 0, keepdims=True)
        dub[:, at] = du.astype(BF16)
    send_parts(tuple(zip(halves(dub), ups)), mine, (s1, s2, s3))


def lnb_kernel(mine, r1, r2, r3, h, gain, prev, e, eb, sums):
    d = (mine[...] + r1[...].astype(F32)) + (r2[...].astype(F32) + r3[...].astype(F32))
    n, inv = norm(h[...])
    w = d * gain[...]
    new = prev[...].astype(F32) + inv * (
        w - jnp.mean(w, -1, keepdims=True) - n * jnp.mean(w * n, -1, keepdims=True)
    )
    e[...] = new
    eb[...] = new.astype(BF16)
    sums[0:1, :] = jnp.sum(d * n, 0, keepdims=True)
    sums[1:2, :] = jnp.sum(d, 0, keepdims=True)
    sums[2:3, :] = jnp.sum(new, 0, keepdims=True)


def attn_back_kernel(e0, e1, e2, e3, *refs):
    wo, wp = sides(refs[:8])
    q, kvf, lse, mask, ef, dq, qsum, keep, send, dmx = refs[8:]
    gather_rows((e0, e1, e2, e3), ef)
    dmx[:, 0:128] = by_rows(ef, wo).astype(BF16)
    dmx[:, 128:256] = by_rows(ef, wp).astype(BF16)
    for h in range(4):
        at = slice(HEAD * h, HEAD * h + HEAD)
        vt = slice(256 + HEAD * h, 256 + HEAD * h + HEAD)
        other = (h + 2) % 4
        at_o = slice(HEAD * other, HEAD * other + HEAD)
        vt_o = slice(256 + HEAD * other, 256 + HEAD * other + HEAD)
        qh, dm = q[:, at], dmx[:, at]
        s = nt(qh * jnp.asarray(0.125, BF16), kvf[:, at]) + mask[...]
        pf = jnp.exp(s - lse[:, h : h + 1])
        dv = tn(pf.astype(BF16), dm)
        keep[:, vt] = dv[0:ROWS, :]
        send[:, vt_o] = dv[ROWS:, :].astype(BF16)
        dp = nt(dm, kvf[:, vt])
        dot = jnp.sum(pf * dp, -1, keepdims=True)
        ds = (pf * (dp - dot) * 0.125).astype(BF16)
        dqh = nn(ds, kvf[:, at])
        qsum[:, at] = jnp.sum(dqh, 0, keepdims=True)
        dq[:, at] = dqh.astype(BF16)
        dk = tn(ds, qh)
        keep[:, at] = dk[0:ROWS, :]
        send[:, at_o] = dk[ROWS:, :].astype(BF16)


def dqkv_kernel(with_sums, dq, keep, recv, *refs):
    ws = sides(refs[:8])
    if with_sums:
        n0, dqkv, vsum, mine, s1, s2, s3, sums = refs[8:]
    else:
        dqkv, vsum, mine, s1, s2, s3 = refs[8:]
    dkv = keep[...] + recv[...].astype(F32)
    vsum[...] = jnp.sum(dkv[:, 256:512], 0, keepdims=True)
    dkv = dkv.astype(BF16)
    for i in range(2):
        at = slice(128 * i, 128 * i + 128)
        base = 384 * i
        dqkv[:, base : base + 128] = dq[:, at]
        dqkv[:, base + 128 : base + 256] = dkv[:, at]
        dqkv[:, base + 256 : base + 384] = dkv[:, 256 + 128 * i : 384 + 128 * i]
    terms = ((dqkv[:, 0:384], ws[0]), (dqkv[:, 384:768], ws[1]))
    for at, total in send_rows(terms, mine, (s1, s2, s3)):
        if with_sums:
            sums[0:1, at] = jnp.sum(total * n0[:, at], 0, keepdims=True)
            sums[1:2, at] = jnp.sum(total, 0, keepdims=True)


def grads_kernel(widths, x1, y1, x2, y2, keep, send):
    w1, w2 = widths
    for out, side in ((send, 1), (keep, 0)):
        out[:, 0:w1] = tn(x1[...], y1[:, side * w1 : side * w1 + w1]).astype(BF16)
        out[:, w1 : w1 + w2] = tn(x2[...], y2[:, side * w2 : side * w2 + w2]).astype(BF16)


def grads_core_kernel(keep, recv, *outs):
    for j, out in enumerate(outs):
        at = slice(256 * j, 256 * j + 256)
        out[...] = (keep[at, :].astype(F32) + recv[at, :].astype(F32)).astype(BF16)


def grads_z_kernel(t, r1, r2, r3, own, other):
    for out, at in ((other, slice(128, 256)), (own, slice(0, 128))):
        t0, t1, t2, t3 = (v[at, :].astype(F32) for v in (t, r1, r2, r3))
        out[...] = ((t0 + t1) + (t2 + t3)).astype(BF16)


def grads_y_kernel(t, r, out):
    out[...] = (t[...].astype(F32) + r[...].astype(F32)).astype(BF16)


def attn_grads_kernel(t0, r0, t1, r1, qkv, out):
    for l, (t, r) in enumerate(((t0, r0), (t1, r1))):
        total = t[...].astype(F32) + r[...].astype(F32)
        for i in range(3):
            qkv[l, i] = total[:, 128 * i : 128 * i + 128]
        out[l] = total[:, 384:512].T


def mlp_grads_kernel(t0, r0, t1, r1, up, down):
    for l, (t, r) in enumerate(((t0, r0), (t1, r1))):
        total = t[...].astype(F32) + r[...].astype(F32)
        up[l] = total[:, 0:512]
        down[l] = total[:, 512:1024].T


def pair_kernel(own, other, pair):
    pair[0:128, :] = own[...]
    pair[128:256, :] = other[...]


def pack_attn_kernel(qkv, out, p0, p1):
    for l, p in enumerate((p0, p1)):
        for i in range(3):
            p[:, 128 * i : 128 * i + 128] = qkv[l, i]
        p[:, 384:512] = out[l].T


def pack_mlp_kernel(up, down, p0, p1):
    for l, p in enumerate((p0, p1)):
        p[:, 0:512] = up[l]
        p[:, 512:1024] = down[l].T


def out_kernel(sc, o0, o1, o2, o3, p0, p1, p2, p3, out):
    cols = columns(sc)
    for core, parts in enumerate(((o0, o1, o2, o3), (p0, p1, p2, p3))):
        for j, part in enumerate(parts):
            g = (sc[0] ^ core) * 4 + (sc[1] ^ j)

            @pl.when(g < 7)
            def _():
                row = pl.multiple_of(g * BLK, BLK)
                for p, col in enumerate(cols):
                    out[pl.ds(row, BLK), pl.ds(col, 128)] = part[
                        :, 128 * p : 128 * p + 128
                    ].astype(F32)

            @pl.when(g == 7)
            def _():
                for p, col in enumerate(cols):
                    out[560:577, pl.ds(col, 128)] = part[0:32, 128 * p : 128 * p + 128].astype(
                        F32
                    )[0:17, :]


def small_x_kernel(k, r1, r2, r3, out):
    out[...] = k[...]
    out[0:12, :] = (k[0:12, :] + r1[0:12, :]) + (r2[0:12, :] + r3[0:12, :])


def small_z_kernel(k, r1, r2, r3, out):
    out[12:16, :] = (k[12:16, :] + r1[12:16, :]) + (r2[12:16, :] + r3[12:16, :])
    for p in range(8):
        a, b, c, d = (slice(128 * (p ^ j), 128 * (p ^ j) + 128) for j in (0, 2, 4, 6))
        out[0:12, a] = (k[0:12, a] + r1[0:12, b]) + (r2[0:12, c] + r3[0:12, d])


def small_y_kernel(k, r, out):
    out[12:16, :] = k[12:16, :] + r[12:16, :]
    for p in range(8):
        a, b = (slice(128 * (p ^ j), 128 * (p ^ j) + 128) for j in (0, 1))
        out[0:12, a] = k[0:12, a] + r[0:12, b]


def small_out_kernel(sc, k, r, out):
    out[12:16, :] = k[12:16, :] + r[12:16, :]
    for p, col in enumerate(columns(sc)):
        a = slice(128 * p, 128 * p + 128)
        out[0:12, pl.ds(col, 128)] = k[0:12, a] + r[0:12, a]


def exchange(x, axis, size, k):
    return lax.ppermute(x, axis, [(i, i ^ k) for i in range(size)])


def core(x):
    return exchange(x, "tp", 8, 1)


def ring_x(xs):
    return [exchange(x, "tp", 8, 2 * (j + 1)) for j, x in enumerate(xs)]


def all_x(x):
    return ring_x((x, x, x))


def ring_z(xs):
    return [exchange(x, "fsdp", 8, 2 * (j + 1)) for j, x in enumerate(xs)]


def flip_y(x):
    return exchange(x, ("rep", "fsdp"), 16, 9)


def pair_up(pack, after=()):
    return call(
        pair_kernel, [((256, pack.shape[1]), BF16)], [pack, flip_y(pack)], after=after
    )[0]


def spread(pair):
    return [pair] + ring_z((pair, pair, pair))


def both_cores(pieces):
    return pieces + [core(p) for p in pieces]


def some(pieces, width, at):
    return [(p, width, at) for p in pieces]


def reduce_core(keep, send):
    width = keep.shape[1]
    return call(grads_core_kernel, [((256, width), BF16)] * 4, [keep, core(send)])


def reduce_z(ts):
    width = ts[0].shape[1]
    return call(grads_z_kernel, [((128, width), BF16)] * 2, [ts[0]] + ring_z(ts[1:]))


def reduce_y(own, other):
    return call(grads_y_kernel, [(own.shape, BF16)], [own, flip_y(other)])[0]


SENDS = [((BLK, 1024), F32)] + [((BLK, 1024), BF16)] * 3


def body(
    images,
    cotangent,
    norm1_gain,
    norm1_shift,
    qkv_weight,
    qv_bias,
    out_weight,
    out_bias,
    norm2_gain,
    norm2_shift,
    up_weight,
    up_bias,
    down_weight,
    down_bias,
):
    tp = lax.axis_index("tp")
    sc = jnp.stack([tp % 2, tp // 2, lax.axis_index("fsdp")]).astype(jnp.int32)
    seq = images.shape[1]

    pa0, pa1 = call(
        pack_attn_kernel,
        [((128, 512), BF16)] * 2,
        [jnp.transpose(qkv_weight, (0, 2, 1, 3)), out_weight],
    )
    pm0, pm1 = call(pack_mlp_kernel, [((128, 1024), BF16)] * 2, [up_weight, down_weight])
    wa0 = spread(pair_up(pa0))
    wm0 = spread(pair_up(pm0, wa0))
    wa1 = spread(pair_up(pa1, wm0))
    pair_m1 = pair_up(pm1, wa1)
    wm1 = spread(pair_m1)
    early1 = wa1
    wa0, wm0, wa1, wm1 = (both_cores(w) for w in (wa0, wm0, wa1, wm1))
    qkv_w = [some(w, 384, 0) for w in (wa0, wa1)]
    out_w = [some(w, 128, 3) for w in (wa0, wa1)]
    up_w = [some(w, 512, 0) for w in (wm0, wm1)]
    down_w = [some(w, 512, 1) for w in (wm0, wm1)]

    mine_small = jnp.concatenate([qv_bias.reshape(2, 256), up_bias], 1)
    other_small = core(mine_small)
    qvb = [
        (mine_small[l, :256].reshape(2, 128), other_small[l, :256].reshape(2, 128))
        for l in range(2)
    ]
    upb = [
        jnp.concatenate([mine_small[l : l + 1, 256:], other_small[l : l + 1, 256:]], 1)
        for l in range(2)
    ]

    rows = jnp.arange(ROWS)
    blocks = (tp // 2) ^ (rows // BLK)
    own = ((tp % 2) * 4 + blocks) * BLK + rows % BLK
    other = ((1 - tp % 2) * 4 + blocks) * BLK + rows % BLK
    mask = jnp.where(jnp.concatenate([own, other]) < seq, 0.0, NEG).astype(F32)[None]

    vec = jnp.concatenate(
        [norm1_gain, norm1_shift, norm2_gain, norm2_shift, out_bias, down_bias], 0
    )
    pad = ((0, 8 * BLK - seq), (0, 0))
    a0, n0, h, eb1, vr, esum = call(
        prep_kernel,
        [
            ((ROWS, 1024), BF16),
            ((ROWS, 1024), F32),
            ((BLK, 1024), F32),
            ((ROWS, 1024), BF16),
            ((12, 1024), F32),
            ((1, 1024), F32),
        ],
        [sc, jnp.pad(images[0], pad), jnp.pad(cotangent[0], pad), vec],
        scratch=[pltpu.VMEM((ROWS, 1024), BF16)],
        smem=1,
    )
    g1, s1v, g2, s2v, ob, db = (
        [vr[2 * i + l : 2 * i + l + 1] for l in range(2)] for i in range(6)
    )

    def attention(parts, l, after=()):
        n = len(parts)
        outs = [((ROWS, 256), BF16), ((ROWS, 512), BF16)]
        if n > 1:
            outs.append(((ROWS, 1024), BF16))
        res = call(
            lambda *refs: qkv_kernel(n, *refs),
            outs,
            list(parts) + qkv_w[l] + [qvb[l][0], qvb[l][1]],
            flops=2 * ROWS * 1024 * 768,
            after=after,
        )
        q, kv = res[0], res[1]
        a_full = res[2] if n > 1 else parts[0]
        mixed, lse, kvf, *sends = call(
            attn_kernel,
            [((ROWS, 256), BF16), ((ROWS, 8), F32), ((2 * ROWS, 512), BF16)] + SENDS,
            [q, kv, core(kv), mask] + out_w[l],
            flops=2 * ROWS * 1024 * 768,
        )
        return q, kvf, lse, mixed, a_full, sends

    def norm_step(sends, prev, bias, gain, shift, after=()):
        return call(
            ln_kernel,
            [((BLK, 1024), F32), ((BLK, 1024), BF16)],
            [sends[0]] + ring_x(sends[1:]) + [prev, bias, gain, shift],
            after=after,
        )

    def norm_back(sends, state, gain, prev, after=()):
        return call(
            lnb_kernel,
            [((BLK, 1024), F32), ((BLK, 1024), BF16), ((3, 1024), F32)],
            [sends[0]] + ring_x(sends[1:]) + [state, gain, prev],
            after=after,
        )

    def attention_back(eb, l, q, kvf, lse, extra, after=(), then=()):
        ef, dq, qsum, keep, send = call(
            attn_back_kernel,
            [
                ((ROWS, 1024), BF16),
                ((ROWS, 256), BF16),
                ((1, 256), F32),
                ((ROWS, 512), F32),
                ((ROWS, 512), BF16),
            ],
            [eb] + all_x(eb) + out_w[l] + [q, kvf, lse, mask],
            flops=4 * ROWS * 1024 * 768,
            scratch=[pltpu.VMEM((ROWS, 256), BF16)],
            after=after,
        )
        outs = [((ROWS, 768), BF16), ((1, 256), F32)] + SENDS
        if extra:
            outs.append(((2, 1024), F32))
        res = call(
            lambda *refs: dqkv_kernel(bool(extra), *refs),
            outs,
            [dq, keep, core(send)] + qkv_w[l] + extra,
            flops=2 * ROWS * 1024 * 768,
            after=then,
        )
        return ef, qsum, res

    def weight_grads(widths, x1, y1, x2, y2):
        shape = ((1024, sum(widths)), BF16)
        return call(
            lambda *refs: grads_kernel(widths, *refs),
            [shape, shape],
            [x1, y1, x2, y2],
            flops=2 * 2 * ROWS * 1024 * sum(widths),
        )

    h_in0 = h
    q0, kvf0, lse0, mixed0, a0, sends = attention([a0], 0)
    h_mid0, b = norm_step(sends, h_in0, ob[0], g2[0], s2v[0])
    z0, slope0, b0, *sends = call(
        mlp_kernel,
        [((ROWS, 1024), BF16), ((ROWS, 1024), F32), ((ROWS, 1024), BF16)] + SENDS,
        [b] + all_x(b) + up_w[0] + down_w[0] + [upb[0]],
        flops=4 * ROWS * 1024 * 1024,
    )
    h_in1, a = norm_step(sends, h_mid0, db[0], g1[1], s1v[1], early1)

    q1, kvf1, lse1, mixed1, a1, sends = attention([a] + all_x(a), 1, [pair_m1])
    h_mid1, b = norm_step(sends, h_in1, ob[1], g2[1], s2v[1])
    z1, dub1, b1, usum1, *sends = call(
        mlp_turn_kernel,
        [((ROWS, 1024), BF16), ((ROWS, 1024), BF16), ((ROWS, 1024), BF16), ((1, 1024), F32)]
        + SENDS,
        [b] + all_x(b) + [eb1] + up_w[1] + down_w[1] + [upb[1]],
        flops=6 * ROWS * 1024 * 1024,
    )

    gm1 = weight_grads((512, 512), b1, dub1, eb1, z1)
    e2, eb, sums21 = norm_back(sends, h_mid1, g2[1], eb1[:BLK], gm1)
    gm1 = reduce_core(*gm1)
    last = call(down_kernel, SENDS, [z1] + down_w[1], flops=2 * ROWS * 1024 * 1024)
    r = [v.astype(F32) for v in ring_x(last[1:])]
    h_out = (h_mid1 + ((last[0] + r[0]) + (r[1] + r[2])) + db[1]).astype(BF16)
    e2f1, qsum1, (dqkv1, vsum1, *sends) = attention_back(
        eb, 1, q1, kvf1, lse1, [], gm1 + last, [h_out]
    )
    ga1 = weight_grads((384, 128), a1, dqkv1, e2f1, mixed1)
    e, eb, sums11 = norm_back(sends, h_in1, g1[1], e2, ga1)
    gm1 = reduce_z(gm1)
    ga1 = reduce_core(*ga1)

    dub0, ebf0, usum0, *sends = call(
        mlp_back_kernel,
        [((ROWS, 1024), BF16), ((ROWS, 1024), BF16), ((1, 1024), F32)] + SENDS,
        [eb] + all_x(eb) + [slope0] + up_w[0] + down_w[0],
        flops=4 * ROWS * 1024 * 1024,
        after=gm1 + ga1,
    )
    gm1 = reduce_y(*gm1)
    gm0 = weight_grads((512, 512), b0, dub0, ebf0, z0)
    e2, eb, sums20 = norm_back(sends, h_mid0, g2[0], e, gm0 + [gm1])
    gm0 = reduce_core(*gm0)
    ga1 = reduce_z(ga1)
    out_parts = [h_out] + all_x(h_out)
    e2f0, qsum0, (dqkv0, vsum0, *sends, sums10) = attention_back(
        eb, 0, q0, kvf0, lse0, [n0], gm0 + ga1, out_parts
    )

    def assemble(parts):
        return call(
            out_kernel, [((seq, 1024), F32)], [sc] + parts + [core(v) for v in parts], smem=1
        )[0]

    out_act = assemble(out_parts)
    ga1 = reduce_y(*ga1)
    ga0 = weight_grads((384, 128), a0, dqkv0, e2f0, mixed0)
    gm0 = reduce_z(gm0)
    e, eb, _ = norm_back(sends, h_in0, g1[0], e2, ga0 + gm0 + [ga1, out_act])
    grad_images = assemble([eb] + all_x(eb))
    ga0 = reduce_y(*reduce_z(reduce_core(*ga0)))
    gm0 = reduce_y(*gm0)
    ga0r, ga1r, gm0r, gm1r = (exchange(t, "rep", 2, 1) for t in (ga0, ga1, gm0, gm1))
    g_qkv, g_out = call(
        attn_grads_kernel,
        [((2, 3, 128, 128), F32), ((2, 128, 128), F32)],
        [ga0, ga0r, ga1, ga1r],
    )
    g_up, g_down = call(
        mlp_grads_kernel,
        [((2, 128, 512), F32), ((2, 512, 128), F32)],
        [gm0, gm0r, gm1, gm1r],
    )

    def tail(side):
        at, up_at = slice(128 * side, 128 * side + 128), slice(512 * side, 512 * side + 512)
        return [
            jnp.concatenate([qs[:, at], vs[:, at], us[:, up_at], jnp.zeros((1, 256), F32)], 1)
            for qs, vs, us in ((qsum0, vsum0, usum0), (qsum1, vsum1, usum1))
        ]

    head = [
        sums10[0:1],
        sums11[0:1],
        sums10[1:2],
        sums11[1:2],
        sums20[0:1],
        sums21[0:1],
        sums20[1:2],
        sums21[1:2],
        sums20[2:3],
        sums21[2:3],
        sums11[2:3],
        esum,
    ]
    blank = [jnp.zeros((2, 1024), F32)]
    small = jnp.concatenate(head + tail(0) + blank, 0)
    small = small + core(jnp.concatenate(head + tail(1) + blank, 0))
    shape = [((16, 1024), F32)]
    small = call(small_x_kernel, shape, [small] + all_x(small))[0]
    small = call(small_z_kernel, shape, [small] + ring_z((small, small, small)))[0]
    small = call(small_y_kernel, shape, [small, flip_y(small)])[0]
    small = call(small_out_kernel, shape, [sc, small, exchange(small, "rep", 2, 1)], smem=1)[0]

    return (
        out_act[None],
        grad_images[None],
        small[0:2],
        small[2:4],
        jnp.transpose(g_qkv, (0, 2, 1, 3)),
        small[12:14, 0:256].reshape(2, 2, 128),
        g_out,
        small[8:10],
        small[4:6],
        small[6:8],
        g_up,
        small[12:14, 256:768],
        g_down,
        small[10:12],
    )


def solution(mesh):
    in_specs = (
        P(("rep", "fsdp"), None, None),
        P(("rep", "fsdp"), None, None),
        P(),
        P(),
        P(None, "fsdp", None, "tp"),
        P(None, None, "tp"),
        P(None, "tp", "fsdp"),
        P(),
        P(),
        P(),
        P(None, "fsdp", "tp"),
        P(None, "tp"),
        P(None, "tp", "fsdp"),
        P(),
    )
    out_specs = (
        P(("rep", "fsdp"), None, None),
        P(("rep", "fsdp"), None, None),
        P(),
        P(),
        P(None, "fsdp", None, "tp"),
        P(None, None, "tp"),
        P(None, "tp", "fsdp"),
        P(),
        P(),
        P(),
        P(None, "fsdp", "tp"),
        P(None, "tp"),
        P(None, "tp", "fsdp"),
        P(),
    )
    return jax.shard_map(body, mesh=mesh, in_specs=in_specs, out_specs=out_specs, check_vma=False)
```

```python
import jax
import jax.numpy as jnp
from jax import lax
from jax.experimental import pallas as pl
from jax.experimental.pallas import tpu as pltpu
from jax.sharding import PartitionSpec as P

F32, BF16 = jnp.float32, jnp.bfloat16
EPSILON = 1e-05
HEAD = 64
BLK = 80
ROWS = 4 * BLK
NEG = -1e30
MIB = 1 << 20


def call(kernel, outs, args, flops=0, scratch=(), smem=0, vmem=40, after=()):
    out_shape = [jax.ShapeDtypeStruct(sh, d) for sh, d in outs]
    specs, arrays, views = [], [], []
    for i, arg in enumerate(args):
        arr, *view = arg if isinstance(arg, tuple) else (arg,)
        place = next((n for n, seen in enumerate(arrays) if seen is arr), len(arrays))
        if place == len(arrays):
            arrays.append(arr)
            specs.append(pl.BlockSpec(memory_space=pltpu.SMEM if i < smem else pltpu.VMEM))
        views.append((place, view))
    nbytes = sum(a.size * a.dtype.itemsize for a in arrays)
    count = len(arrays)
    specs += [pl.BlockSpec(memory_space=pl.ANY)] * len(after)

    def run(*refs):
        ins = [
            refs[n].at[:, view[0] * view[1] : view[0] * (view[1] + 1)] if view else refs[n]
            for n, view in views
        ]
        kernel(*ins, *refs[count + len(after) :])

    return list(
        pl.pallas_call(
            run,
            out_shape=out_shape,
            in_specs=specs,
            out_specs=[pl.BlockSpec(memory_space=pltpu.VMEM)] * len(outs),
            scratch_shapes=list(scratch),
            compiler_params=pltpu.CompilerParams(vmem_limit_bytes=vmem * MIB),
            cost_estimate=pl.CostEstimate(flops=1024, bytes_accessed=1024, transcendentals=0),
        )(*arrays, *after)
    )


def nn(a, b):
    return lax.dot_general(a, b, (((1,), (0,)), ((), ())), preferred_element_type=F32)


def nt(a, b):
    return lax.dot_general(a, b, (((1,), (1,)), ((), ())), preferred_element_type=F32)


def tn(a, b):
    return lax.dot_general(a, b, (((0,), (0,)), ((), ())), preferred_element_type=F32)


def by_rows(a, pieces):
    total = None
    for j, w in enumerate(pieces):
        part = nn(a[:, 256 * j : 256 * j + 256], w[...])
        total = part if total is None else total + part
    return total


def norm(v):
    mean = jnp.mean(v, -1, keepdims=True)
    cen = v - mean
    inv = lax.rsqrt(jnp.mean(cen * cen, -1, keepdims=True) + EPSILON)
    return cen * inv, inv


def gelu(u):
    cdf = 0.5 * (1.0 + lax.erf(u * 0.7071067811865476))
    pdf = jnp.exp(-0.5 * u * u) * 0.3989422804014327
    return u * cdf, cdf + u * pdf


def columns(sc):
    return [pl.multiple_of((sc[2] ^ p) * 128, 128) for p in range(8)]


def prep_kernel(sc, img, cot, vec, a0, n0, h0, eb, vout, esum, ims):
    cols = columns(sc)
    for p, col in enumerate(cols):
        vout[:, 128 * p : 128 * p + 128] = vec[:, pl.ds(col, 128)]
    for j in range(4):
        row = pl.multiple_of((sc[0] * 4 + (sc[1] ^ j)) * BLK, BLK)
        for p, col in enumerate(cols):
            here = (slice(BLK * j, BLK * j + BLK), slice(128 * p, 128 * p + 128))
            there = (pl.ds(row, BLK), pl.ds(col, 128))
            ims[here] = img[there]
            eb[here] = cot[there]
    h0[...] = ims[0:BLK, :].astype(F32)
    esum[...] = jnp.sum(eb[0:BLK, :].astype(F32), 0, keepdims=True)
    gain, shift = vout[0:1, :], vout[2:3, :]
    for j in range(4):
        rows = slice(BLK * j, BLK * j + BLK)
        n, _ = norm(ims[rows, :].astype(F32))
        n0[rows, :] = n
        a0[rows, :] = (n * gain + shift).astype(BF16)


def gather_rows(parts, full):
    for j, part in enumerate(parts):
        full[BLK * j : BLK * j + BLK, :] = part[...]


def sides(refs):
    return refs[0:4], refs[4:8]


def send_rows(terms, mine, sends):
    for j in range(4):
        at = slice(256 * j, 256 * j + 256)
        total = None
        for x, pieces in terms:
            part = nt(x, pieces[j][...])
            total = part if total is None else total + part
        mine[:, at] = total[0:BLK, :]
        for i, send in enumerate(sends):
            send[0:BLK, at] = total[BLK * (i + 1) : BLK * (i + 2), :].astype(BF16)
        yield at, total


def send_parts(terms, mine, sends):
    for _ in send_rows(terms, mine, sends):
        pass


def qkv_kernel(nparts, *refs):
    parts, (wo, wp), (bo, bp), (q, kv), rest = (
        refs[:nparts],
        sides(refs[nparts : nparts + 8]),
        refs[nparts + 8 : nparts + 10],
        refs[nparts + 10 : nparts + 12],
        refs[nparts + 12 :],
    )
    a = parts[0]
    if nparts > 1:
        gather_rows(parts, rest[0])
        a = rest[0]
    for i, (w, b) in enumerate(((wo, bo), (wp, bp))):
        y = by_rows(a, w)
        at = slice(128 * i, 128 * i + 128)
        q[:, at] = (y[:, 0:128] + b[0:1, :]).astype(BF16)
        kv[:, at] = y[:, 128:256].astype(BF16)
        kv[:, 256 + 128 * i : 384 + 128 * i] = (y[:, 256:384] + b[1:2, :]).astype(BF16)


def swap128(ref):
    for i, j in enumerate((1, 0, 3, 2)):
        yield slice(128 * i, 128 * i + 128), slice(128 * j, 128 * j + 128)


def attn_kernel(q, kv, kvp, mask, *refs):
    wo, wp = sides(refs[:8])
    mixed, lse, kvf, mine, s1, s2, s3 = refs[8:]
    kvf[0:ROWS, :] = kv[...]
    for here, there in swap128(kvp):
        kvf[ROWS:, here] = kvp[:, there]
    for h in range(4):
        at = slice(HEAD * h, HEAD * h + HEAD)
        qh = q[:, at] * jnp.asarray(0.125, BF16)
        s = nt(qh, kvf[:, at]) + mask[...]
        top = jnp.max(s, -1, keepdims=True)
        e = jnp.exp(s - top)
        tot = jnp.sum(e, -1, keepdims=True)
        lse[:, h : h + 1] = top + jnp.log(tot)
        out = nn(e.astype(BF16), kvf[:, 256 + HEAD * h : 256 + HEAD * h + HEAD])
        mixed[:, at] = (out * (1.0 / tot)).astype(BF16)
    send_parts(((mixed[:, 0:128], wo), (mixed[:, 128:256], wp)), mine, (s1, s2, s3))


def ln_kernel(mine, r1, r2, r3, prev, bias, gain, shift, h, b):
    v = prev[...] + (
        (mine[...] + r1[...].astype(F32)) + (r2[...].astype(F32) + r3[...].astype(F32))
    ) + bias[...]
    h[...] = v
    n, _ = norm(v)
    b[...] = (n * gain[...] + shift[...]).astype(BF16)


def halves(x):
    return x[:, 0:512], x[:, 512:1024]


def mlp_kernel(b0, b1, b2, b3, *refs):
    ups, downs = sides(refs[:8]), sides(refs[8:16])
    bias, z, slope, bf, mine, s1, s2, s3 = refs[16:]
    gather_rows((b0, b1, b2, b3), bf)
    for i in range(2):
        at = slice(512 * i, 512 * i + 512)
        zz, sl = gelu(by_rows(bf, ups[i]) + bias[:, at])
        slope[:, at] = sl
        z[:, at] = zz.astype(BF16)
    send_parts(tuple(zip(halves(z), downs)), mine, (s1, s2, s3))


def mlp_turn_kernel(b0, b1, b2, b3, eb, *refs):
    ups, downs = sides(refs[:8]), sides(refs[8:16])
    bias, z, dub, bf, usum, mine, s1, s2, s3 = refs[16:]
    gather_rows((b0, b1, b2, b3), bf)
    for i in range(2):
        at = slice(512 * i, 512 * i + 512)
        zz, sl = gelu(by_rows(bf, ups[i]) + bias[:, at])
        z[:, at] = zz.astype(BF16)
        du = by_rows(eb, downs[i]) * sl
        usum[:, at] = jnp.sum(du, 0, keepdims=True)
        dub[:, at] = du.astype(BF16)
    send_parts(tuple(zip(halves(dub), ups)), mine, (s1, s2, s3))


def down_kernel(z, *refs):
    mine, s1, s2, s3 = refs[8:]
    send_parts(tuple(zip(halves(z), sides(refs[:8]))), mine, (s1, s2, s3))


def mlp_back_kernel(e0, e1, e2, e3, slope, *refs):
    ups, downs = sides(refs[:8]), sides(refs[8:16])
    dub, ebf, usum, mine, s1, s2, s3 = refs[16:]
    gather_rows((e0, e1, e2, e3), ebf)
    for i in range(2):
        at = slice(512 * i, 512 * i + 512)
        du = by_rows(ebf, downs[i]) * slope[:, at]
        usum[:, at] = jnp.sum(du, 0, keepdims=True)
        dub[:, at] = du.astype(BF16)
    send_parts(tuple(zip(halves(dub), ups)), mine, (s1, s2, s3))


def lnb_kernel(mine, r1, r2, r3, h, gain, prev, e, eb, sums):
    r1, r2, r3 = (r[0:BLK, :].astype(F32) for r in (r1, r2, r3))
    d = (mine[...] + r1) + (r2 + r3)
    n, inv = norm(h[...])
    w = d * gain[...]
    new = prev[...].astype(F32) + inv * (
        w - jnp.mean(w, -1, keepdims=True) - n * jnp.mean(w * n, -1, keepdims=True)
    )
    e[...] = new
    eb[...] = new.astype(BF16)
    sums[0:1, :] = jnp.sum(d * n, 0, keepdims=True)
    sums[1:2, :] = jnp.sum(d, 0, keepdims=True)
    sums[2:3, :] = jnp.sum(new, 0, keepdims=True)


def attn_back_kernel(e0, e1, e2, e3, *refs):
    wo, wp = sides(refs[:8])
    q, kvf, lse, mask, ef, dq, qsum, keep, send, dmx = refs[8:]
    gather_rows((e0, e1, e2, e3), ef)
    dmx[:, 0:128] = by_rows(ef, wo).astype(BF16)
    dmx[:, 128:256] = by_rows(ef, wp).astype(BF16)
    for h in range(4):
        at = slice(HEAD * h, HEAD * h + HEAD)
        vt = slice(256 + HEAD * h, 256 + HEAD * h + HEAD)
        other = (h + 2) % 4
        at_o = slice(HEAD * other, HEAD * other + HEAD)
        vt_o = slice(256 + HEAD * other, 256 + HEAD * other + HEAD)
        qh, dm = q[:, at], dmx[:, at]
        s = nt(qh * jnp.asarray(0.125, BF16), kvf[:, at]) + mask[...]
        pf = jnp.exp(s - lse[:, h : h + 1])
        dv = tn(pf.astype(BF16), dm)
        keep[:, vt] = dv[0:ROWS, :]
        send[:, vt_o] = dv[ROWS:, :].astype(BF16)
        dp = nt(dm, kvf[:, vt])
        dot = jnp.sum(pf * dp, -1, keepdims=True)
        ds = (pf * (dp - dot) * 0.125).astype(BF16)
        dqh = nn(ds, kvf[:, at])
        qsum[:, at] = jnp.sum(dqh, 0, keepdims=True)
        dq[:, at] = dqh.astype(BF16)
        dk = tn(ds, qh)
        keep[:, at] = dk[0:ROWS, :]
        send[:, at_o] = dk[ROWS:, :].astype(BF16)


def dqkv_kernel(with_sums, dq, keep, recv, *refs):
    ws = sides(refs[:8])
    if with_sums:
        n0, m0, m1, n1, esum, qs0, qs1, vs1, us0, us1 = refs[8:18]
        dqkv, vsum, mine, s1, s2, s3, small = refs[18:]
    else:
        dqkv, vsum, mine, s1, s2, s3 = refs[8:]
    dkv = keep[...] + recv[...].astype(F32)
    vsum[...] = jnp.sum(dkv[:, 256:512], 0, keepdims=True)
    dkv = dkv.astype(BF16)
    for i in range(2):
        at = slice(128 * i, 128 * i + 128)
        base = 384 * i
        dqkv[:, base : base + 128] = dq[:, at]
        dqkv[:, base + 128 : base + 256] = dkv[:, at]
        dqkv[:, base + 256 : base + 384] = dkv[:, 256 + 128 * i : 384 + 128 * i]
    terms = ((dqkv[:, 0:384], ws[0]), (dqkv[:, 384:768], ws[1]))
    for at, total in send_rows(terms, mine, (s1, s2, s3)):
        if with_sums:
            small[0:1, at] = jnp.sum(total * n0[:, at], 0, keepdims=True)
            small[2:3, at] = jnp.sum(total, 0, keepdims=True)
    if with_sums:
        rows = (
            (1, n1, 0), (3, n1, 1), (4, m0, 0), (5, m1, 0), (6, m0, 1), (7, m1, 1),
            (8, m0, 2), (9, m1, 2), (10, n1, 2), (11, esum, 0),
        )
        for i, ref, row in rows:
            small[i : i + 1, :] = ref[row : row + 1, :]
        small[12:16, :] = jnp.zeros((4, 1024), F32)
        for l, (q, v, u) in enumerate(((qs0, vsum, us0), (qs1, vs1, us1))):
            for side in range(2):
                i = 12 + 2 * side + l
                at = slice(128 * side, 128 * side + 128)
                small[i : i + 1, 0:128] = q[:, at]
                small[i : i + 1, 128:256] = v[:, at]
                small[i : i + 1, 256:768] = u[:, 512 * side : 512 * side + 512]
        rounded = small[...].astype(BF16)
        small[...] = rounded.astype(F32)
        for send in (s1, s2, s3):
            send[BLK : BLK + 16, :] = rounded


def grads_kernel(widths, x1, y1, x2, y2, keep, send):
    w1, w2 = widths
    for out, side in ((send, 1), (keep, 0)):
        out[:, 0:w1] = tn(x1[...], y1[:, side * w1 : side * w1 + w1]).astype(BF16)
        out[:, w1 : w1 + w2] = tn(x2[...], y2[:, side * w2 : side * w2 + w2]).astype(BF16)


def grads_core_kernel(keep, recv, *outs):
    for j, out in enumerate(outs):
        at = slice(256 * j, 256 * j + 256)
        out[...] = (keep[at, :].astype(F32) + recv[at, :].astype(F32)).astype(BF16)


def grads_z_kernel(t, r1, r2, r3, own, other):
    for out, at in ((other, slice(128, 256)), (own, slice(0, 128))):
        t0, t1, t2, t3 = (v[at, :].astype(F32) for v in (t, r1, r2, r3))
        out[...] = ((t0 + t1) + (t2 + t3)).astype(BF16)


def grads_y_kernel(t, r, out):
    out[...] = (t[...].astype(F32) + r[...].astype(F32)).astype(BF16)


def attn_grads_kernel(t0, r0, t1, r1, qkv, out):
    for l, (t, r) in enumerate(((t0, r0), (t1, r1))):
        total = t[...].astype(F32) + r[...].astype(F32)
        for i in range(3):
            qkv[l, i] = total[:, 128 * i : 128 * i + 128]
        out[l] = total[:, 384:512].T


def mlp_grads_kernel(t0, r0, t1, r1, up, down):
    for l, (t, r) in enumerate(((t0, r0), (t1, r1))):
        total = t[...].astype(F32) + r[...].astype(F32)
        up[l] = total[:, 0:512]
        down[l] = total[:, 512:1024].T


def pair_kernel(own, other, pair):
    pair[0:128, :] = own[...]
    pair[128:256, :] = other[...]


def pack_attn_kernel(qkv, out, p0, p1):
    for l, p in enumerate((p0, p1)):
        for i in range(3):
            p[:, 128 * i : 128 * i + 128] = qkv[l, i]
        p[:, 384:512] = out[l].T


def pack_mlp_kernel(up, down, p0, p1):
    for l, p in enumerate((p0, p1)):
        p[:, 0:512] = up[l]
        p[:, 512:1024] = down[l].T


def out_kernel(sc, o0, o1, o2, o3, p0, p1, p2, p3, out):
    for core, parts in enumerate(((o0, o1, o2, o3), (p0, p1, p2, p3))):
        for j, part in enumerate(parts):
            g = (sc[0] ^ core) * 4 + (sc[1] ^ j)

            @pl.when(g < 7)
            def _():
                for p in range(8):
                    first = g * (8 * BLK) + (sc[2] ^ p)
                    out[pl.ds(first, BLK, stride=8), :] = part[
                        :, 128 * p : 128 * p + 128
                    ].astype(F32)

            @pl.when(g == 7)
            def _():
                for p in range(8):
                    first = 7 * (8 * BLK) + (sc[2] ^ p)
                    out[pl.ds(first, 17, stride=8), :] = part[
                        0:32, 128 * p : 128 * p + 128
                    ].astype(F32)[0:17, :]


def small_x_kernel(k, r1, r2, r3, out):
    r1, r2, r3 = (r[BLK : BLK + 16, :].astype(F32) for r in (r1, r2, r3))
    out[...] = k[...]
    out[0:12, :] = (k[0:12, :] + r1[0:12, :]) + (r2[0:12, :] + r3[0:12, :])


def small_core_kernel(k, r, out):
    out[0:12, :] = k[0:12, :] + r[0:12, :]
    out[12:14, :] = k[12:14, :] + r[14:16, :]
    out[14:16, :] = jnp.zeros((2, 1024), F32)


def small_z_kernel(k, r1, r2, r3, out):
    out[12:16, :] = (k[12:16, :] + r1[12:16, :]) + (r2[12:16, :] + r3[12:16, :])
    for p in range(8):
        a, b, c, d = (slice(128 * (p ^ j), 128 * (p ^ j) + 128) for j in (0, 2, 4, 6))
        out[0:12, a] = (k[0:12, a] + r1[0:12, b]) + (r2[0:12, c] + r3[0:12, d])


def small_y_kernel(k, r, out):
    out[12:16, :] = k[12:16, :] + r[12:16, :]
    for p in range(8):
        a, b = (slice(128 * (p ^ j), 128 * (p ^ j) + 128) for j in (0, 1))
        out[0:12, a] = k[0:12, a] + r[0:12, b]


def small_out_kernel(sc, k, r, out):
    out[12:16, :] = k[12:16, :] + r[12:16, :]
    for p, col in enumerate(columns(sc)):
        a = slice(128 * p, 128 * p + 128)
        out[0:12, pl.ds(col, 128)] = k[0:12, a] + r[0:12, a]


def exchange(x, axis, size, k):
    return lax.ppermute(x, axis, [(i, i ^ k) for i in range(size)])


def core(x):
    return exchange(x, "tp", 8, 1)


def ring_x(xs):
    return [exchange(x, "tp", 8, 2 * (j + 1)) for j, x in enumerate(xs)]


def all_x(x):
    return ring_x((x, x, x))


def ring_z(xs):
    return [exchange(x, "fsdp", 8, 2 * (j + 1)) for j, x in enumerate(xs)]


def flip_y(x):
    return exchange(x, ("rep", "fsdp"), 16, 9)


def pair_up(pack, after=(), other=None):
    return call(
        pair_kernel, [((256, pack.shape[1]), BF16)], [pack, flip_y(pack) if other is None else other], after=after
    )[0]


def spread(pair):
    return [pair] + ring_z((pair, pair, pair))


def both_cores(pieces):
    return pieces + [core(p) for p in pieces]


def some(pieces, width, at):
    return [(p, width, at) for p in pieces]


def reduce_core(keep, send):
    width = keep.shape[1]
    return call(grads_core_kernel, [((256, width), BF16)] * 4, [keep, core(send)])


def reduce_z(ts):
    width = ts[0].shape[1]
    return call(grads_z_kernel, [((128, width), BF16)] * 2, [ts[0]] + ring_z(ts[1:]))


def reduce_y(own, other):
    return call(grads_y_kernel, [(own.shape, BF16)], [own, flip_y(other)])[0]


SENDS = [((BLK, 1024), F32)] + [((BLK, 1024), BF16)] * 3


def body(
    images,
    cotangent,
    norm1_gain,
    norm1_shift,
    qkv_weight,
    qv_bias,
    out_weight,
    out_bias,
    norm2_gain,
    norm2_shift,
    up_weight,
    up_bias,
    down_weight,
    down_bias,
):
    tp = lax.axis_index("tp")
    sc = jnp.stack([tp % 2, tp // 2, lax.axis_index("fsdp")]).astype(jnp.int32)
    seq = images.shape[1]

    mine_small = jnp.concatenate([qv_bias.reshape(2, 256), up_bias], 1)
    other_small = core(mine_small)
    qvb = [
        (mine_small[l, :256].reshape(2, 128), other_small[l, :256].reshape(2, 128))
        for l in range(2)
    ]
    upb = [
        jnp.concatenate([mine_small[l : l + 1, 256:], other_small[l : l + 1, 256:]], 1)
        for l in range(2)
    ]

    rows = jnp.arange(ROWS)
    blocks = (tp // 2) ^ (rows // BLK)
    own = ((tp % 2) * 4 + blocks) * BLK + rows % BLK
    other = ((1 - tp % 2) * 4 + blocks) * BLK + rows % BLK
    mask = jnp.where(jnp.concatenate([own, other]) < seq, 0.0, NEG).astype(F32)[None]

    vec = jnp.concatenate(
        [norm1_gain, norm1_shift, norm2_gain, norm2_shift, out_bias, down_bias], 0
    )
    pad = ((0, 8 * BLK - seq), (0, 0))
    a0, n0, h, eb1, vr, esum = call(
        prep_kernel,
        [
            ((ROWS, 1024), BF16),
            ((ROWS, 1024), F32),
            ((BLK, 1024), F32),
            ((ROWS, 1024), BF16),
            ((12, 1024), F32),
            ((1, 1024), F32),
        ],
        [sc, jnp.pad(images[0], pad), jnp.pad(cotangent[0], pad), vec],
        scratch=[pltpu.VMEM((ROWS, 1024), BF16)],
        smem=1,
    )
    g1, s1v, g2, s2v, ob, db = (
        [vr[2 * i + l : 2 * i + l + 1] for l in range(2)] for i in range(6)
    )

    pa0, pa1 = call(
        pack_attn_kernel,
        [((128, 512), BF16)] * 2,
        [jnp.transpose(qkv_weight, (0, 2, 1, 3)), out_weight],
    )
    pair = pair_up(pa0, [a0])
    wa0 = spread(pair)
    pm0, pm1 = call(
        pack_mlp_kernel, [((128, 1024), BF16)] * 2, [up_weight, down_weight], after=[pair]
    )
    wm0 = spread(pair_up(pm0, wa0))
    wa1 = spread(pair_up(pa1, wm0))
    pair_m1 = pair_up(pm1, wa1)
    wm1 = spread(pair_m1)
    early1 = wa1
    wa0, wm0, wa1, wm1 = (both_cores(w) for w in (wa0, wm0, wa1, wm1))
    qkv_w = [some(w, 384, 0) for w in (wa0, wa1)]
    out_w = [some(w, 128, 3) for w in (wa0, wa1)]
    up_w = [some(w, 512, 0) for w in (wm0, wm1)]
    down_w = [some(w, 512, 1) for w in (wm0, wm1)]

    def attention(parts, l, after=()):
        n = len(parts)
        outs = [((ROWS, 256), BF16), ((ROWS, 512), BF16)]
        if n > 1:
            outs.append(((ROWS, 1024), BF16))
        res = call(
            lambda *refs: qkv_kernel(n, *refs),
            outs,
            list(parts) + qkv_w[l] + [qvb[l][0], qvb[l][1]],
            flops=2 * ROWS * 1024 * 768,
            after=after,
        )
        q, kv = res[0], res[1]
        a_full = res[2] if n > 1 else parts[0]
        mixed, lse, kvf, *sends = call(
            attn_kernel,
            [((ROWS, 256), BF16), ((ROWS, 8), F32), ((2 * ROWS, 512), BF16)] + SENDS,
            [q, kv, core(kv), mask] + out_w[l],
            flops=2 * ROWS * 1024 * 768,
        )
        return q, kvf, lse, mixed, a_full, sends

    def norm_step(sends, prev, bias, gain, shift, after=()):
        return call(
            ln_kernel,
            [((BLK, 1024), F32), ((BLK, 1024), BF16)],
            [sends[0]] + ring_x(sends[1:]) + [prev, bias, gain, shift],
            after=after,
        )

    def norm_back(sends, state, gain, prev, after=(), r=None):
        r = ring_x(sends[1:]) if r is None else r
        return call(
            lnb_kernel,
            [((BLK, 1024), F32), ((BLK, 1024), BF16), ((3, 1024), F32)],
            [sends[0]] + r + [state, gain, prev],
            after=after,
        )

    def attention_back(eb, l, q, kvf, lse, extra, after=(), then=()):
        ef, dq, qsum, keep, send = call(
            attn_back_kernel,
            [
                ((ROWS, 1024), BF16),
                ((ROWS, 256), BF16),
                ((1, 256), F32),
                ((ROWS, 512), F32),
                ((ROWS, 512), BF16),
            ],
            [eb] + all_x(eb) + out_w[l] + [q, kvf, lse, mask],
            flops=4 * ROWS * 1024 * 768,
            scratch=[pltpu.VMEM((ROWS, 256), BF16)],
            after=after,
        )
        outs = [((ROWS, 768), BF16), ((1, 256), F32)] + SENDS
        if extra:
            outs[3:] = [((BLK + 16, 1024), BF16)] * 3 + [((16, 1024), F32)]
            extra = extra + [qsum]
            extra.insert(5, extra.pop())
        res = call(
            lambda *refs: dqkv_kernel(bool(extra), *refs),
            outs,
            [dq, keep, core(send)] + qkv_w[l] + extra,
            flops=2 * ROWS * 1024 * 768,
            after=then,
        )
        return ef, qsum, res

    def weight_grads(widths, x1, y1, x2, y2):
        shape = ((1024, sum(widths)), BF16)
        return call(
            lambda *refs: grads_kernel(widths, *refs),
            [shape, shape],
            [x1, y1, x2, y2],
            flops=2 * 2 * ROWS * 1024 * sum(widths),
        )

    h_in0 = h
    q0, kvf0, lse0, mixed0, a0, sends = attention([a0], 0)
    h_mid0, b = norm_step(sends, h_in0, ob[0], g2[0], s2v[0])
    z0, slope0, b0, *sends = call(
        mlp_kernel,
        [((ROWS, 1024), BF16), ((ROWS, 1024), F32), ((ROWS, 1024), BF16)] + SENDS,
        [b] + all_x(b) + up_w[0] + down_w[0] + [upb[0]],
        flops=4 * ROWS * 1024 * 1024,
    )
    h_in1, a = norm_step(sends, h_mid0, db[0], g1[1], s1v[1], early1)

    q1, kvf1, lse1, mixed1, a1, sends = attention([a] + all_x(a), 1, [pair_m1])
    h_mid1, b = norm_step(sends, h_in1, ob[1], g2[1], s2v[1])
    z1, dub1, b1, usum1, *sends = call(
        mlp_turn_kernel,
        [((ROWS, 1024), BF16), ((ROWS, 1024), BF16), ((ROWS, 1024), BF16), ((1, 1024), F32)]
        + SENDS,
        [b] + all_x(b) + [eb1] + up_w[1] + down_w[1] + [upb[1]],
        flops=6 * ROWS * 1024 * 1024,
    )

    gm1 = weight_grads((512, 512), b1, dub1, eb1, z1)
    e2, eb, sums21 = norm_back(sends, h_mid1, g2[1], eb1[:BLK], gm1[1:])
    gm1 = reduce_core(*gm1)
    last = call(down_kernel, SENDS, [z1] + down_w[1], flops=2 * ROWS * 1024 * 1024)
    r = [v.astype(F32) for v in ring_x(last[1:])]
    h_out = (h_mid1 + ((last[0] + r[0]) + (r[1] + r[2])) + db[1]).astype(BF16)
    e2f1, qsum1, (dqkv1, vsum1, *sends) = attention_back(
        eb, 1, q1, kvf1, lse1, [], [gm1[1], last[1]], [h_out]
    )
    ga1 = weight_grads((384, 128), a1, dqkv1, e2f1, mixed1)
    e, eb, sums11 = norm_back(sends, h_in1, g1[1], e2, ga1[1:])
    gm1 = reduce_z(gm1)
    ga1 = reduce_core(*ga1)

    dub0, ebf0, usum0, *sends = call(
        mlp_back_kernel,
        [((ROWS, 1024), BF16), ((ROWS, 1024), BF16), ((1, 1024), F32)] + SENDS,
        [eb] + all_x(eb) + [slope0] + up_w[0] + down_w[0],
        flops=4 * ROWS * 1024 * 1024,
        after=[gm1[1], ga1[1]],
    )
    gm1 = reduce_y(*gm1)
    gm0 = weight_grads((512, 512), b0, dub0, ebf0, z0)
    e2, eb, sums20 = norm_back(sends, h_mid0, g2[0], e, [gm0[1], gm1])
    gm0 = reduce_core(*gm0)
    ga1 = reduce_z(ga1)
    out_parts = [h_out] + all_x(h_out)
    e2f0, _, (dqkv0, _, *sends, small) = attention_back(
        eb, 0, q0, kvf0, lse0, [n0, sums20, sums21, sums11, esum, qsum1, vsum1, usum0, usum1], [gm0[1], ga1[1]], out_parts[1:]
    )

    def assemble(parts):
        return call(
            out_kernel, [((8 * seq, 128), F32)], [sc] + parts + [core(v) for v in parts], smem=1
        )[0].reshape(1, seq, 1024)

    out_act = assemble(out_parts)
    ga1 = reduce_y(*ga1)
    ga0 = weight_grads((384, 128), a0, dqkv0, e2f0, mixed0)
    gm0 = reduce_z(gm0)
    r = ring_x(sends[1:])
    shape = [((16, 1024), F32)]
    small = call(small_x_kernel, shape, [small] + r)[0]
    e, eb, _ = norm_back(sends, h_in0, g1[0], e2, (), r)
    grad_images = assemble([eb] + all_x(eb))
    ga0 = reduce_y(*reduce_z(reduce_core(*ga0)))
    gm0 = reduce_y(*gm0)
    ga0r, ga1r, gm0r, gm1r = (exchange(t, "rep", 2, 1) for t in (ga0, ga1, gm0, gm1))
    g_qkv, g_out = call(
        attn_grads_kernel,
        [((2, 3, 128, 128), F32), ((2, 128, 128), F32)],
        [ga0, ga0r, ga1, ga1r],
    )
    g_up, g_down = call(
        mlp_grads_kernel,
        [((2, 128, 512), F32), ((2, 512, 128), F32)],
        [gm0, gm0r, gm1, gm1r],
    )

    small = call(small_core_kernel, shape, [small, core(small)])[0]
    small = call(small_z_kernel, shape, [small] + ring_z((small, small, small)))[0]
    small = call(small_y_kernel, shape, [small, flip_y(small)])[0]
    small = call(small_out_kernel, shape, [sc, small, exchange(small, "rep", 2, 1)], smem=1)[0]

    return (
        out_act,
        grad_images,
        small[0:2],
        small[2:4],
        jnp.transpose(g_qkv, (0, 2, 1, 3)),
        small[12:14, 0:256].reshape(2, 2, 128),
        g_out,
        small[8:10],
        small[4:6],
        small[6:8],
        g_up,
        small[12:14, 256:768],
        g_down,
        small[10:12],
    )


def solution(mesh):
    in_specs = (
        P(("rep", "fsdp"), None, None),
        P(("rep", "fsdp"), None, None),
        P(),
        P(),
        P(None, "fsdp", None, "tp"),
        P(None, None, "tp"),
        P(None, "tp", "fsdp"),
        P(),
        P(),
        P(),
        P(None, "fsdp", "tp"),
        P(None, "tp"),
        P(None, "tp", "fsdp"),
        P(),
    )
    out_specs = (
        P(("rep", "fsdp"), None, None),
        P(("rep", "fsdp"), None, None),
        P(),
        P(),
        P(None, "fsdp", None, "tp"),
        P(None, None, "tp"),
        P(None, "tp", "fsdp"),
        P(),
        P(),
        P(),
        P(None, "fsdp", "tp"),
        P(None, "tp"),
        P(None, "tp", "fsdp"),
        P(),
    )
    return jax.shard_map(body, mesh=mesh, in_specs=in_specs, out_specs=out_specs, check_vma=False)
```
